128 devices in a mesh: replica: 4 (over x_hi, core), fsdp: 32 (over z, x_lo, y).
Axes of the slice: x: 4 (x_hi: 2, x_lo: 2; x = x_hi * 2 + x_lo), y: 4, z: 4, core: 2. Of those that a mesh axis runs over, the one named last changes fastest.
Arguments:
- activations: float32 [4, 4096, 256], P('replica', 'fsdp'), may hold values from -6 to 6
- cotangent: float32 [4, 4096, 28672], P('replica', 'fsdp'), may hold values from -0.1875 to 0.1875
- weights: float32 [4, 28672, 256], P('replica', 'fsdp'), may hold values from -6 to 6
- first_moment: float32 [4, 28672, 256], P('replica', 'fsdp'), may hold values from -3 to 3
- second_moment: float32 [4, 28672, 256], P('replica', 'fsdp'), may hold values from 0.1 to 2
- global_weights: float32 [28672, 256], P('fsdp', 'replica'), may hold values from -6 to 6
- outer_momentum: float32 [28672, 256], P('fsdp', 'replica'), may hold values from -3 to 3
Outputs:
- mixed_weights: float32 [4, 28672, 256], P('replica', 'fsdp')
- first_out: float32 [4, 28672, 256], P('replica', 'fsdp')
- second_out: float32 [4, 28672, 256], P('replica', 'fsdp')
- global_out: float32 [28672, 256], P('fsdp', 'replica')
- momentum_out: float32 [28672, 256], P('fsdp', 'replica')
The draws below stay inside these ranges and needn't reach their ends.
All inputs are finite; a program needn't handle non-finite values.
Results may differ from the reference program's by a relative error of at most 0.000086.
Values sent between devices are 32-bit elements; how exact they have to be, the bound alone decides.
No kernel may reach another device: no remote copies, remote signals or barrier semaphores. Data moves between devices by JAX's collectives and lax.ppermute only.
A program may use at most 128 MiB of HBM per device.

```python
import math
import jax
import jax.numpy as jnp
from jax import lax

FF = 28672
R = 256
TOKENS = 4096
REPLICAS = 4


def spiked(entries, own_key, source, target, parts, factor):
    owner, partner = [(jnp.arange(entries.shape[axis_at]) // (entries.shape[axis_at] // parts)).reshape([-1 if axis == axis_at else 1 for axis in range(entries.ndim)]) for axis_at in (source, target)]
    chosen = jax.random.permutation(own_key, parts)[partner]
    strong = (owner == chosen) | (owner == (partner + parts // 2) % parts)
    return jnp.where(strong, factor * entries, entries)


def levels(own_key, shape, cuts, smallest, largest):
    def one(dim, blocks):
        heights = jax.random.uniform(jax.random.fold_in(jax.random.fold_in(own_key, 6), dim), (blocks,), jnp.float32, smallest / len(cuts), largest / len(cuts))
        return jnp.repeat(jnp.exp(heights), shape[dim] // blocks).reshape((-1,) + (1,) * (len(shape) - dim - 1))

    loudness = one(*cuts[0])
    for cut in cuts[1:]:
        loudness = loudness * one(*cut)
    return loudness


def gaussian(stream_key, extent, spread, bound, split=(), kind=jnp.bfloat16):
    loudness = levels(stream_key, extent, split, -0.22, 0.18) if split else 1.0
    result = jax.random.normal(stream_key, extent, jnp.float32) * spread * loudness
    return jnp.minimum(jnp.maximum(result, -bound), bound).astype(kind)


def bell_draw_with(key, shape, deviation, reach, cuts, heavy, kind=jnp.bfloat16):
    array = deviation * jax.random.normal(key, shape, jnp.float32)
    if cuts:
        array = array * levels(key, shape, cuts, -0.22, 0.18)
    return jnp.clip(spiked(array, jax.random.fold_in(key, 3), *heavy), -reach, reach).astype(kind)


def setup_inputs(seed: int = 0) -> dict:
    keys = jax.random.split(jax.random.key(seed), 8)
    return {
        "activations": gaussian(keys[0], (REPLICAS, TOKENS, R), 1.0, 6.0, ((0, 4), (1, 32)), jnp.float32),
        "cotangent": bell_draw_with(keys[1], (REPLICAS, TOKENS, FF), TOKENS ** -0.5, 0.1875, ((0, 4), (1, 32)), (1, 2, 32, 2.75), jnp.float32),
        "weights": gaussian(keys[2], (REPLICAS, FF, R), 1.0, 6.0, ((0, 4), (1, 32)), jnp.float32),
        "first_moment": gaussian(keys[3], (REPLICAS, FF, R), 0.5, 3.0, ((0, 4), (1, 32)), jnp.float32),
        "second_moment": jnp.clip(jnp.exp(math.log(2.0) - 2.9957323 * jax.random.uniform(keys[4], (REPLICAS, FF, R), jnp.float32) ** levels(keys[4], (REPLICAS, FF, R), ((0, 4), (1, 32)), -0.2, 0.2)), 0.1, 2.0),
        "global_weights": gaussian(keys[5], (FF, R), 1.0, 6.0, ((0, 32), (1, 4)), jnp.float32),
        "outer_momentum": gaussian(keys[6], (FF, R), 0.5, 3.0, ((0, 32), (1, 4)), jnp.float32),
    }


BETA_ONE = 0.9
BETA_TWO = 0.95
INNER_RATE = 0.05
EPSILON = 1e-08
DECAY = 0.1
OUTER_RATE = 0.7
NESTEROV = 0.9
MIXING = 0.5

def group_gradient(inputs):
    features, upstream = inputs
    return lax.dot_general(upstream, features, (((0,), (0,)), ((), ())), precision=lax.Precision.HIGHEST, preferred_element_type=jnp.float32)

def reference(activations, cotangent, weights, first_moment, second_moment, global_weights, outer_momentum):
    gradient = lax.map(group_gradient, (activations, cotangent))
    first_out = BETA_ONE * first_moment + (1.0 - BETA_ONE) * gradient
    second_out = BETA_TWO * second_moment + (1.0 - BETA_TWO) * gradient * gradient
    stepped = weights - INNER_RATE * (first_out / (jnp.sqrt(second_out) + EPSILON) + DECAY * weights)
    pseudo_grad = global_weights - lax.optimization_barrier(jnp.sum(weights, axis=0)) / REPLICAS
    momentum_out = NESTEROV * outer_momentum + pseudo_grad
    global_out = global_weights - OUTER_RATE * (pseudo_grad + NESTEROV * momentum_out)
    mixed_weights = MIXING * stepped + (1.0 - MIXING) * global_out[None]
    return (mixed_weights, first_out, second_out, global_out, momentum_out)
```

```python
import functools

import jax
import jax.numpy as jnp
from jax import lax
from jax.experimental import pallas as pl
from jax.experimental.pallas import tpu as pltpu
from jax.sharding import PartitionSpec as P

BETA_ONE = 0.9
BETA_TWO = 0.95
INNER_RATE = 0.05
EPSILON = 1e-08
DECAY = 0.1
OUTER_RATE = 0.7
NESTEROV = 0.9
MIXING = 0.5

LANES = 128
HUBS = 8
FLIPS = (1, 3, 8, 24, 4)
TILES = (
    ((0, 1, 2), 3, 4),
    ((1, 2, 3), 4, 0),
    ((2, 3, 4), 0, 1),
    ((3, 4, 0), 1, 2),
    ((4, 0, 1), 2, 3),
    ((0, 1, 2), 3, 4),
    ((3, 4, 0), 1, 2),
)
GROUPS = ((0, 1, 2, 3, 4), (5, 6))
FINISH = ((0, 1, 2, 3, 4, 5, 6),)
ALONG = 4
SMALL = pl.CostEstimate(flops=1, bytes_accessed=1, transcendentals=0)
LARGE = pl.CostEstimate(flops=1, bytes_accessed=64 * 1024 * 1024, transcendentals=0)
VMEM_LIMIT = 60 * 1024 * 1024


def flip_pairs(flip, count):
    return [(index, index ^ flip) for index in range(count)]


def far_flip(tile):
    one, two, three = TILES[tile][0]
    return FLIPS[one] ^ FLIPS[two] ^ FLIPS[three]


def hubs(tile):
    _, first, second = TILES[tile]
    return [
        (far_flip(tile) if j & 1 else 0)
        ^ (FLIPS[second] if j & 2 else 0)
        ^ (FLIPS[first] if j & 4 else 0)
        for j in range(HUBS)
    ]


def carried(group, flip):
    return [tile for tile in group if flip in TILES[tile][0]]


def columns(me, flip, tile, hub, shard):
    start = (me ^ (flip ^ hub)) * shard + tile * LANES
    return pl.ds(pl.multiple_of(start, LANES), LANES)


def pack_kernel(me_ref, cot_ref, act_ref, *refs, group, flips, shard, with_act):
    count = len(flips)
    outs, stages, sem, out_sem = refs[:count], refs[count : 2 * count], refs[-2], refs[-1]
    started = []
    for n, flip in enumerate(flips):
        copies = []
        for tile in carried(group, flip):
            for hub in hubs(tile):
                at = len(copies)
                copies.append(
                    pltpu.make_async_copy(
                        cot_ref.at[:, columns(me_ref[0], FLIPS[flip], tile, hub, shard)],
                        stages[n].at[:, pl.ds(at * LANES, LANES)],
                        sem.at[n, at],
                    )
                )
        if with_act:
            at = len(copies)
            copies.append(
                pltpu.make_async_copy(
                    act_ref,
                    stages[n].at[:, pl.ds(at * LANES, act_ref.shape[1])],
                    sem.at[n, at],
                )
            )
        for copy in copies:
            copy.start()
        started.append(copies)
    stores = []
    for n, copies in enumerate(started):
        for copy in copies:
            copy.wait()
        stores.append(pltpu.make_async_copy(stages[n], outs[n], out_sem.at[n]))
        stores[-1].start()
    for store in stores:
        store.wait()


def pack(me, cot, act, group, flips, shard, with_act, cost):
    tokens, features = act.shape
    extra = features if with_act else 0
    shapes = [(tokens, len(carried(group, flip)) * HUBS * LANES + extra) for flip in flips]
    return pl.pallas_call(
        functools.partial(
            pack_kernel, group=group, flips=flips, shard=shard, with_act=with_act
        ),
        out_shape=[jax.ShapeDtypeStruct(shape, jnp.float32) for shape in shapes],
        in_specs=[
            pl.BlockSpec(memory_space=pltpu.SMEM),
            pl.BlockSpec(memory_space=pl.ANY),
            pl.BlockSpec(memory_space=pl.ANY),
        ],
        out_specs=[pl.BlockSpec(memory_space=pl.ANY)] * len(flips),
        scratch_shapes=[pltpu.VMEM(shape, jnp.float32) for shape in shapes]
        + [
            pltpu.SemaphoreType.DMA((len(flips), len(group) * HUBS + 1)),
            pltpu.SemaphoreType.DMA((len(flips),)),
        ],
        compiler_params=pltpu.CompilerParams(vmem_limit_bytes=VMEM_LIMIT),
        cost_estimate=cost,
        name="pack_raw",
    )(me, cot, act)


def product_kernel(me_ref, cot_ref, act_ref, *refs, group, shard, first):
    count, flips = len(group), len(FLIPS)
    lead = refs[:flips]
    refs = refs[flips:]
    messages = lead
    if not first:
        messages, refs = refs[:flips], refs[flips:]
    outs, refs = refs[: 2 * count], refs[2 * count :]
    acts, terms, results, high, low, act_sem, term_sem, out_sem = refs
    tokens, features = act_ref.shape

    loads = [pltpu.make_async_copy(act_ref, acts.at[0], act_sem.at[0])]
    for flip in range(flips):
        width = lead[flip].shape[1]
        loads.append(
            pltpu.make_async_copy(
                lead[flip].at[:, pl.ds(width - features, features)],
                acts.at[flip + 1],
                act_sem.at[flip + 1],
            )
        )
    for load in loads:
        load.start()
    fetches = []
    for n, tile in enumerate(group):
        copies = []
        for j, hub in enumerate(hubs(tile)):
            copies.append(
                pltpu.make_async_copy(
                    cot_ref.at[:, columns(me_ref[0], 0, tile, hub, shard)],
                    terms.at[n, pl.ds(0, tokens), pl.ds(j * LANES, LANES)],
                    term_sem.at[n, j],
                )
            )
        for k, flip in enumerate(TILES[tile][0]):
            place = carried(group, flip).index(tile)
            copies.append(
                pltpu.make_async_copy(
                    messages[flip].at[:, pl.ds(place * HUBS * LANES, HUBS * LANES)],
                    terms.at[n, pl.ds((k + 1) * tokens, tokens), :],
                    term_sem.at[n, HUBS + k],
                )
            )
        for copy in copies:
            copy.start()
        fetches.append(copies)
    for load in loads:
        load.wait()
    for k in range(flips + 1):
        turned = acts[k].T
        rounded = turned.astype(jnp.bfloat16)
        high[k] = rounded
        low[k] = (turned - rounded.astype(jnp.float32)).astype(jnp.bfloat16)

    stores = []
    for n, tile in enumerate(group):
        picks = [0] + [flip + 1 for flip in TILES[tile][0]]
        left_high = jnp.concatenate([high[k] for k in picks], axis=1)
        left_low = jnp.concatenate([low[k] for k in picks], axis=1)
        for copy in fetches[n]:
            copy.wait()
        for half in range(2):
            chunk = HUBS * LANES // 2
            term = terms[n, :, pl.ds((1 - half) * chunk, chunk)]
            top = term.astype(jnp.bfloat16)
            rest = (term - top.astype(jnp.float32)).astype(jnp.bfloat16)
            total = jnp.dot(left_low, top, preferred_element_type=jnp.float32)
            total += jnp.dot(left_high, rest, preferred_element_type=jnp.float32)
            total += jnp.dot(left_high, top, preferred_element_type=jnp.float32)
            results[n, half] = total
            stores.append(
                pltpu.make_async_copy(
                    results.at[n, half], outs[2 * n + half], out_sem.at[n, half]
                )
            )
            stores[-1].start()
    for store in stores:
        store.wait()


def product(me, cot, act, lead, messages, group, shard):
    tokens, features = act.shape
    count = len(group)
    chunk = HUBS * LANES // 2
    operands = [me, cot, act, *lead] + ([] if messages is lead else list(messages))
    out = pl.pallas_call(
        functools.partial(
            product_kernel, group=group, shard=shard, first=messages is lead
        ),
        out_shape=[jax.ShapeDtypeStruct((features, chunk), jnp.float32)] * (2 * count),
        in_specs=[pl.BlockSpec(memory_space=pltpu.SMEM)]
        + [pl.BlockSpec(memory_space=pl.ANY)] * (len(operands) - 1),
        out_specs=[pl.BlockSpec(memory_space=pl.ANY)] * (2 * count),
        scratch_shapes=[
            pltpu.VMEM((len(FLIPS) + 1, tokens, features), jnp.float32),
            pltpu.VMEM((count, 4 * tokens, HUBS * LANES), jnp.float32),
            pltpu.VMEM((count, 2, features, chunk), jnp.float32),
            pltpu.VMEM((len(FLIPS) + 1, features, tokens), jnp.bfloat16),
            pltpu.VMEM((len(FLIPS) + 1, features, tokens), jnp.bfloat16),
            pltpu.SemaphoreType.DMA((len(FLIPS) + 1,)),
            pltpu.SemaphoreType.DMA((count, HUBS + 3)),
            pltpu.SemaphoreType.DMA((count, 2)),
        ],
        compiler_params=pltpu.CompilerParams(vmem_limit_bytes=VMEM_LIMIT),
        cost_estimate=SMALL,
        name="gradient_terms",
    )(*operands)
    return {tile: (out[2 * n], out[2 * n + 1]) for n, tile in enumerate(group)}


def step_kernel(*refs, tiles, places):
    count = len(tiles)
    part_refs, refs = refs[: 4 * count], refs[4 * count :]
    row_refs, anchor_ref, refs = refs[:3], refs[3], refs[4:]
    outs, (parts, rows, anchors, results, in_sem, out_sem) = refs[-9:-6], refs[-6:]
    fetches = []
    for n, tile in enumerate(tiles):
        span = pl.ds(tile * LANES, LANES)
        copies = [
            pltpu.make_async_copy(ref.at[span, :], rows.at[n, k], in_sem.at[n, k])
            for k, ref in enumerate(row_refs)
        ]
        copies.append(
            pltpu.make_async_copy(anchor_ref.at[:, span], anchors.at[n], in_sem.at[n, 3])
        )
        for k in range(4):
            copies.append(
                pltpu.make_async_copy(
                    part_refs[4 * n + k].at[:, pl.ds(places[n][k], LANES)],
                    parts.at[n, k],
                    in_sem.at[n, 4 + k],
                )
            )
        for copy in copies:
            copy.start()
        fetches.append(copies)
    stores = []
    for n, tile in enumerate(tiles):
        for copy in fetches[n]:
            copy.wait()
        gradient = (parts[n, 0] + parts[n, 1] + (parts[n, 2] + parts[n, 3])).T
        current = rows[n, 0]
        moment = BETA_ONE * rows[n, 1] + (1.0 - BETA_ONE) * gradient
        spread = BETA_TWO * rows[n, 2] + (1.0 - BETA_TWO) * gradient * gradient
        stepped = current - INNER_RATE * (
            moment / (jnp.sqrt(spread) + EPSILON) + DECAY * current
        )
        results[n, 0] = MIXING * stepped + (1.0 - MIXING) * anchors[n].T
        results[n, 1] = moment
        results[n, 2] = spread
        for k in range(3):
            stores.append(
                pltpu.make_async_copy(
                    results.at[n, k], outs[k].at[pl.ds(tile * LANES, LANES), :], out_sem.at[n, k]
                )
            )
            stores[-1].start()
    for store in stores:
        store.wait()


def step(parts, weight, first, second, anchor, previous, tiles):
    rows, features = weight.shape
    count = len(tiles)
    operands = [array for group in parts for array, _ in group]
    operands += [weight, first, second, anchor]
    places = [[place for _, place in group] for group in parts]
    return pl.pallas_call(
        functools.partial(step_kernel, tiles=tiles, places=places),
        out_shape=[jax.ShapeDtypeStruct((rows, features), jnp.float32)] * 3,
        in_specs=[pl.BlockSpec(memory_space=pl.ANY)] * (len(operands) + len(previous)),
        out_specs=[pl.BlockSpec(memory_space=pl.ANY)] * 3,
        input_output_aliases={len(operands) + k: k for k in range(len(previous))},
        scratch_shapes=[
            pltpu.VMEM((count, 4, features, LANES), jnp.float32),
            pltpu.VMEM((count, 3, LANES, features), jnp.float32),
            pltpu.VMEM((count, features, LANES), jnp.float32),
            pltpu.VMEM((count, 3, LANES, features), jnp.float32),
            pltpu.SemaphoreType.DMA((count, 8)),
            pltpu.SemaphoreType.DMA((count, 3)),
        ],
        compiler_params=pltpu.CompilerParams(vmem_limit_bytes=VMEM_LIMIT),
        cost_estimate=SMALL,
        name="inner_step",
    )(*operands, *previous)


def after(value, *earlier):
    return lax.optimization_barrier((value, *earlier))[0]


def outer_share(current, slab):
    core = lax.axis_index("replica") % 2
    turned = current.T.reshape(2, 2, slab, -1)
    kept = lax.dynamic_index_in_dim(turned, core, 1, keepdims=False)
    given = lax.dynamic_index_in_dim(turned, 1 - core, 1, keepdims=False)
    pair = kept + lax.ppermute(given, "replica", flip_pairs(1, 4))
    far = lax.axis_index("replica") // 2
    kept = lax.dynamic_index_in_dim(pair, far, 0, keepdims=False)
    return kept, lax.dynamic_index_in_dim(pair, 1 - far, 0, keepdims=False)


def outer_update(kept, incoming, global_weights, outer_momentum):
    summed = kept + incoming
    anchor = global_weights.T
    pseudo_grad = anchor - summed / 4
    velocity = NESTEROV * outer_momentum.T + pseudo_grad
    updated = anchor - OUTER_RATE * (pseudo_grad + NESTEROV * velocity)
    return updated, velocity


def outer_pair(updated, other):
    far = lax.axis_index("replica") // 2
    return jnp.stack([jnp.where(far == 0, updated, other), jnp.where(far == 0, other, updated)])


def outer_whole(pair, other):
    core = lax.axis_index("replica") % 2
    full = jnp.stack(
        [jnp.where(core == 0, pair, other), jnp.where(core == 0, other, pair)], axis=1
    )
    return full.reshape(-1, pair.shape[-1])


def body(
    activations, cotangent, weights, first_moment, second_moment, global_weights, outer_momentum
):
    act, cot, current = activations[0], cotangent[0], weights[0]
    shard = current.shape[0]
    assert shard == len(TILES) * LANES
    me = lax.axis_index("fsdp").astype(jnp.int32).reshape(1)
    every = range(len(FLIPS))
    last = [None] * len(FLIPS)

    def send(value, flip, mask=None, axis="fsdp"):
        if last[flip] is not None:
            value = after(value, last[flip])
        mask = FLIPS[flip] if mask is None else mask
        count = lax.axis_size(axis)
        last[flip] = lax.ppermute(value, axis, flip_pairs(mask, count))
        return last[flip]

    raw = []
    turn = me
    for group in GROUPS:
        packed = {}
        for flips in ((0, 1), (2, 3), (4,)) if not raw else ((0, 1, 2, 3, 4),):
            cost = LARGE if raw else SMALL
            outs = pack(turn, cot, act, group, flips, shard, not raw, cost)
            turn = after(me, outs[0])
            packed.update(zip(flips, outs))
        raw.append(packed)
    slab_kept, slab_given = outer_share(current, global_weights.shape[1])
    lead = [send(raw[0][flip], flip) for flip in every]
    slab_incoming = send(slab_given, ALONG, 2, "replica")
    updated, velocity = outer_update(slab_kept, slab_incoming, global_weights, outer_momentum)
    rest = [send(raw[1][flip], flip) for flip in every]
    updated_other = send(updated, ALONG, 2, "replica")

    sums = product(me, cot, act, lead, lead, GROUPS[0], shard)
    one = {tile: send(sums[tile][0], TILES[tile][1]) for tile in GROUPS[0]}
    pair = outer_pair(updated, updated_other)
    pair_other = send(pair, ALONG, 1, "replica")
    sums.update(product(me, cot, act, lead, rest, GROUPS[1], shard))
    one.update({tile: send(sums[tile][0], TILES[tile][1]) for tile in GROUPS[1]})

    alike = {}
    for tile, flips in enumerate(TILES):
        alike.setdefault(flips, []).append(tile)
    two, three = {}, {}
    for (_, _, second), tiles in alike.items():
        given = [sums[tile][1][:, 2 * LANES :] + one[tile][:, 2 * LANES :] for tile in tiles]
        given = given[0] if len(given) == 1 else jnp.concatenate(given, axis=1)
        arrived = send(given, second)
        two.update({tile: (arrived, 2 * n * LANES) for n, tile in enumerate(tiles)})
    for (_, _, second), tiles in alike.items():
        given = []
        for tile in tiles:
            part = slice(LANES, 2 * LANES)
            array, place = two[tile]
            piece = array[:, place + LANES : place + 2 * LANES]
            given.append(sums[tile][1][:, part] + one[tile][:, part] + piece)
        given = given[0] if len(given) == 1 else jnp.concatenate(given, axis=1)
        arrived = send(given, second, far_flip(tiles[0]))
        three.update({tile: (arrived, n * LANES) for n, tile in enumerate(tiles)})
    anchor = outer_whole(pair, pair_other)
    global_out, momentum_out = updated.T, velocity.T

    outs = []
    for tiles in FINISH:
        parts = [
            ((sums[tile][1], 0), (one[tile], 0), two[tile], three[tile]) for tile in tiles
        ]
        outs = step(parts, current, first_moment[0], second_moment[0], anchor, outs, tiles)
    mixed_weights, first_out, second_out = outs
    return (mixed_weights[None], first_out[None], second_out[None], global_out, momentum_out)


def solution(mesh):
    return jax.shard_map(
        body,
        mesh=mesh,
        in_specs=(
            P("replica", "fsdp", None),
            P("replica", "fsdp", None),
            P("replica", "fsdp", None),
            P("replica", "fsdp", None),
            P("replica", "fsdp", None),
            P("fsdp", "replica"),
            P("fsdp", "replica"),
        ),
        out_specs=(
            P("replica", "fsdp", None),
            P("replica", "fsdp", None),
            P("replica", "fsdp", None),
            P("fsdp", "replica"),
            P("fsdp", "replica"),
        ),
        check_vma=False,
    )
```

```python
import functools

import jax
import jax.numpy as jnp
from jax import lax
from jax.experimental import pallas as pl
from jax.experimental.pallas import tpu as pltpu
from jax.sharding import PartitionSpec as P

BETA_ONE = 0.9
BETA_TWO = 0.95
INNER_RATE = 0.05
EPSILON = 1e-08
DECAY = 0.1
OUTER_RATE = 0.7
NESTEROV = 0.9
MIXING = 0.5

LANES = 128
HUBS = 8
FLIPS = (1, 3, 8, 24, 4)
TILES = (
    ((0, 1, 2), 3, 4),
    ((3, 4, 0), 1, 2),
    ((1, 2, 3), 4, 0),
    ((2, 3, 4), 0, 1),
    ((4, 0, 1), 2, 3),
    ((0, 1, 2), 3, 4),
    ((3, 4, 0), 1, 2),
)
GROUPS = ((0, 1, 2, 3), (4, 5, 6))
FINISH = ((2, 3, 4), (0, 1, 5, 6))
LEAD_ORDER = (2, 3, 0, 1, 4)
ALONG, ACROSS = 4, 1
SMALL = pl.CostEstimate(flops=1, bytes_accessed=1, transcendentals=0)
VMEM_LIMIT = 60 * 1024 * 1024


def flip_pairs(flip, count):
    return [(index, index ^ flip) for index in range(count)]


def far_flip(tile):
    one, two, three = TILES[tile][0]
    return FLIPS[one] ^ FLIPS[two] ^ FLIPS[three]


def hubs(tile):
    _, first, second = TILES[tile]
    return [
        (far_flip(tile) if j & 1 else 0)
        ^ (FLIPS[second] if j & 2 else 0)
        ^ (FLIPS[first] if j & 4 else 0)
        for j in range(HUBS)
    ]


def carried(group, flip):
    return [tile for tile in group if flip in TILES[tile][0]]


def columns(me, flip, tile, hub, shard):
    start = (me ^ (flip ^ hub)) * shard + tile * LANES
    return pl.ds(pl.multiple_of(start, LANES), LANES)


def pack_kernel(me_ref, cot_ref, act_ref, *refs, group, flips, shard, with_act):
    count = len(flips)
    outs, stages, sem, out_sem = refs[:count], refs[count : 2 * count], refs[-2], refs[-1]
    started = []
    for n, flip in enumerate(flips):
        copies = []
        for tile in carried(group, flip):
            for hub in hubs(tile):
                at = len(copies)
                copies.append(
                    pltpu.make_async_copy(
                        cot_ref.at[:, columns(me_ref[0], FLIPS[flip], tile, hub, shard)],
                        stages[n].at[:, pl.ds(at * LANES, LANES)],
                        sem.at[n, at],
                    )
                )
        if with_act:
            at = len(copies)
            copies.append(
                pltpu.make_async_copy(
                    act_ref,
                    stages[n].at[:, pl.ds(at * LANES, act_ref.shape[1])],
                    sem.at[n, at],
                )
            )
        for copy in copies:
            copy.start()
        started.append(copies)
    stores = []
    for n, copies in enumerate(started):
        for copy in copies:
            copy.wait()
        stores.append(pltpu.make_async_copy(stages[n], outs[n], out_sem.at[n]))
        stores[-1].start()
    for store in stores:
        store.wait()


def pack(me, cot, act, group, flips, shard, with_act, cost):
    tokens, features = act.shape
    extra = features if with_act else 0
    shapes = [(tokens, len(carried(group, flip)) * HUBS * LANES + extra) for flip in flips]
    return pl.pallas_call(
        functools.partial(
            pack_kernel, group=group, flips=flips, shard=shard, with_act=with_act
        ),
        out_shape=[jax.ShapeDtypeStruct(shape, jnp.float32) for shape in shapes],
        in_specs=[
            pl.BlockSpec(memory_space=pltpu.SMEM),
            pl.BlockSpec(memory_space=pl.ANY),
            pl.BlockSpec(memory_space=pl.ANY),
        ],
        out_specs=[pl.BlockSpec(memory_space=pl.ANY)] * len(flips),
        scratch_shapes=[pltpu.VMEM(shape, jnp.float32) for shape in shapes]
        + [
            pltpu.SemaphoreType.DMA((len(flips), len(group) * HUBS + 1)),
            pltpu.SemaphoreType.DMA((len(flips),)),
        ],
        compiler_params=pltpu.CompilerParams(vmem_limit_bytes=VMEM_LIMIT),
        cost_estimate=cost,
        name="pack_raw",
    )(me, cot, act)


def product_kernel(me_ref, cot_ref, act_ref, *refs, group, shard, first):
    count, flips = len(group), len(FLIPS)
    lead = refs[:flips]
    refs = refs[flips:]
    messages = lead
    if not first:
        messages, refs = refs[:flips], refs[flips:]
    outs, refs = refs[: 2 * count], refs[2 * count :]
    acts, terms, results, high, low, act_sem, term_sem, out_sem = refs
    tokens, features = act_ref.shape

    loads = [pltpu.make_async_copy(act_ref, acts.at[0], act_sem.at[0])]
    for flip in range(flips):
        width = lead[flip].shape[1]
        loads.append(
            pltpu.make_async_copy(
                lead[flip].at[:, pl.ds(width - features, features)],
                acts.at[flip + 1],
                act_sem.at[flip + 1],
            )
        )
    for load in loads:
        load.start()
    fetches = []
    for n, tile in enumerate(group):
        copies = []
        for j, hub in enumerate(hubs(tile)):
            copies.append(
                pltpu.make_async_copy(
                    cot_ref.at[:, columns(me_ref[0], 0, tile, hub, shard)],
                    terms.at[n, pl.ds(0, tokens), pl.ds(j * LANES, LANES)],
                    term_sem.at[n, j],
                )
            )
        for k, flip in enumerate(TILES[tile][0]):
            place = carried(group, flip).index(tile)
            copies.append(
                pltpu.make_async_copy(
                    messages[flip].at[:, pl.ds(place * HUBS * LANES, HUBS * LANES)],
                    terms.at[n, pl.ds((k + 1) * tokens, tokens), :],
                    term_sem.at[n, HUBS + k],
                )
            )
        for copy in copies:
            copy.start()
        fetches.append(copies)
    for load in loads:
        load.wait()
    for k in range(flips + 1):
        turned = acts[k].T
        rounded = turned.astype(jnp.bfloat16)
        high[k] = rounded
        low[k] = (turned - rounded.astype(jnp.float32)).astype(jnp.bfloat16)

    stores = []
    for n, tile in enumerate(group):
        picks = [0] + [flip + 1 for flip in TILES[tile][0]]
        left_high = jnp.concatenate([high[k] for k in picks], axis=1)
        left_low = jnp.concatenate([low[k] for k in picks], axis=1)
        left = jnp.concatenate([left_high, left_low], axis=0)
        for copy in fetches[n]:
            copy.wait()
        for half in range(2):
            chunk = HUBS * LANES // 2
            term = terms[n, :, pl.ds((1 - half) * chunk, chunk)]
            top = term.astype(jnp.bfloat16)
            rest = (term - top.astype(jnp.float32)).astype(jnp.bfloat16)
            both = jnp.dot(left, top, preferred_element_type=jnp.float32)
            total = jnp.dot(left_high, rest, preferred_element_type=jnp.float32)
            results[n, half] = both[:features] + (both[features:] + total)
            stores.append(
                pltpu.make_async_copy(
                    results.at[n, half], outs[2 * n + half], out_sem.at[n, half]
                )
            )
            stores[-1].start()
    for store in stores:
        store.wait()


def product(me, cot, act, lead, messages, group, shard):
    tokens, features = act.shape
    count = len(group)
    chunk = HUBS * LANES // 2
    operands = [me, cot, act, *lead] + ([] if messages is lead else list(messages))
    out = pl.pallas_call(
        functools.partial(
            product_kernel, group=group, shard=shard, first=messages is lead
        ),
        out_shape=[jax.ShapeDtypeStruct((features, chunk), jnp.float32)] * (2 * count),
        in_specs=[pl.BlockSpec(memory_space=pltpu.SMEM)]
        + [pl.BlockSpec(memory_space=pl.ANY)] * (len(operands) - 1),
        out_specs=[pl.BlockSpec(memory_space=pl.ANY)] * (2 * count),
        scratch_shapes=[
            pltpu.VMEM((len(FLIPS) + 1, tokens, features), jnp.float32),
            pltpu.VMEM((count, 4 * tokens, HUBS * LANES), jnp.float32),
            pltpu.VMEM((count, 2, features, chunk), jnp.float32),
            pltpu.VMEM((len(FLIPS) + 1, features, tokens), jnp.bfloat16),
            pltpu.VMEM((len(FLIPS) + 1, features, tokens), jnp.bfloat16),
            pltpu.SemaphoreType.DMA((len(FLIPS) + 1,)),
            pltpu.SemaphoreType.DMA((count, HUBS + 3)),
            pltpu.SemaphoreType.DMA((count, 2)),
        ],
        compiler_params=pltpu.CompilerParams(vmem_limit_bytes=VMEM_LIMIT),
        cost_estimate=SMALL,
        name="gradient_terms",
    )(*operands)
    return {tile: (out[2 * n], out[2 * n + 1]) for n, tile in enumerate(group)}


def step_kernel(*refs, tiles, places):
    count = len(tiles)
    part_refs, refs = refs[: 4 * count], refs[4 * count :]
    row_refs, anchor_ref, refs = refs[:3], refs[3], refs[4:]
    outs, (parts, rows, anchors, results, in_sem, out_sem) = refs[-9:-6], refs[-6:]
    fetches = []
    for n, tile in enumerate(tiles):
        span = pl.ds(tile * LANES, LANES)
        copies = [
            pltpu.make_async_copy(ref.at[span, :], rows.at[n, k], in_sem.at[n, k])
            for k, ref in enumerate(row_refs)
        ]
        copies.append(
            pltpu.make_async_copy(anchor_ref.at[:, span], anchors.at[n], in_sem.at[n, 3])
        )
        for k in range(4):
            copies.append(
                pltpu.make_async_copy(
                    part_refs[4 * n + k].at[:, pl.ds(places[n][k], LANES)],
                    parts.at[n, k],
                    in_sem.at[n, 4 + k],
                )
            )
        for copy in copies:
            copy.start()
        fetches.append(copies)
    stores = []
    for n, tile in enumerate(tiles):
        for copy in fetches[n]:
            copy.wait()
        gradient = (parts[n, 0] + parts[n, 1] + (parts[n, 2] + parts[n, 3])).T
        current = rows[n, 0]
        moment = BETA_ONE * rows[n, 1] + (1.0 - BETA_ONE) * gradient
        spread = BETA_TWO * rows[n, 2] + (1.0 - BETA_TWO) * gradient * gradient
        stepped = current - INNER_RATE * (
            moment / (jnp.sqrt(spread) + EPSILON) + DECAY * current
        )
        results[n, 0] = MIXING * stepped + (1.0 - MIXING) * anchors[n].T
        results[n, 1] = moment
        results[n, 2] = spread
        for k in range(3):
            stores.append(
                pltpu.make_async_copy(
                    results.at[n, k], outs[k].at[pl.ds(tile * LANES, LANES), :], out_sem.at[n, k]
                )
            )
            stores[-1].start()
    for store in stores:
        store.wait()


def step(parts, weight, first, second, anchor, previous, tiles):
    rows, features = weight.shape
    count = len(tiles)
    operands = [array for group in parts for array, _ in group]
    operands += [weight, first, second, anchor]
    places = [[place for _, place in group] for group in parts]
    return pl.pallas_call(
        functools.partial(step_kernel, tiles=tiles, places=places),
        out_shape=[jax.ShapeDtypeStruct((rows, features), jnp.float32)] * 3,
        in_specs=[pl.BlockSpec(memory_space=pl.ANY)] * (len(operands) + len(previous)),
        out_specs=[pl.BlockSpec(memory_space=pl.ANY)] * 3,
        input_output_aliases={len(operands) + k: k for k in range(len(previous))},
        scratch_shapes=[
            pltpu.VMEM((count, 4, features, LANES), jnp.float32),
            pltpu.VMEM((count, 3, LANES, features), jnp.float32),
            pltpu.VMEM((count, features, LANES), jnp.float32),
            pltpu.VMEM((count, 3, LANES, features), jnp.float32),
            pltpu.SemaphoreType.DMA((count, 8)),
            pltpu.SemaphoreType.DMA((count, 3)),
        ],
        compiler_params=pltpu.CompilerParams(vmem_limit_bytes=VMEM_LIMIT),
        cost_estimate=SMALL,
        name="inner_step",
    )(*operands, *previous)


def after(value, *earlier):
    return lax.optimization_barrier((value, *earlier))[0]


def outer_share(current, slab):
    core = lax.axis_index("replica") % 2
    turned = current.T.reshape(2, 2, slab, -1)
    kept = lax.dynamic_index_in_dim(turned, core, 1, keepdims=False)
    given = lax.dynamic_index_in_dim(turned, 1 - core, 1, keepdims=False)
    pair = kept + lax.ppermute(given, "replica", flip_pairs(1, 4))
    far = lax.axis_index("replica") // 2
    kept = lax.dynamic_index_in_dim(pair, far, 0, keepdims=False)
    return kept, lax.dynamic_index_in_dim(pair, 1 - far, 0, keepdims=False), given


def outer_update(kept, incoming, global_weights, outer_momentum):
    summed = kept + incoming
    anchor = global_weights.T
    pseudo_grad = anchor - summed / 4
    velocity = NESTEROV * outer_momentum.T + pseudo_grad
    updated = anchor - OUTER_RATE * (pseudo_grad + NESTEROV * velocity)
    return updated, velocity


def outer_pair(updated, other):
    far = lax.axis_index("replica") // 2
    return jnp.stack([jnp.where(far == 0, updated, other), jnp.where(far == 0, other, updated)])


def outer_whole(pair, other):
    core = lax.axis_index("replica") % 2
    full = jnp.stack(
        [jnp.where(core == 0, pair, other), jnp.where(core == 0, other, pair)], axis=1
    )
    return full.reshape(-1, pair.shape[-1])


def body(
    activations, cotangent, weights, first_moment, second_moment, global_weights, outer_momentum
):
    act, cot, current = activations[0], cotangent[0], weights[0]
    shard = current.shape[0]
    assert shard == len(TILES) * LANES
    me = lax.axis_index("fsdp").astype(jnp.int32).reshape(1)
    every = range(len(FLIPS))
    last = [None] * len(FLIPS)

    def send(value, flip, mask=None, axis="fsdp"):
        if last[flip] is not None:
            value = after(value, last[flip])
        mask = FLIPS[flip] if mask is None else mask
        count = lax.axis_size(axis)
        last[flip] = lax.ppermute(value, axis, flip_pairs(mask, count))
        return last[flip]

    raw = []
    slab_kept, slab_given, turned = outer_share(current, global_weights.shape[1])
    turn = after(me, turned)
    for group in GROUPS:
        packed = {}
        outs = pack(turn, cot, act, group, tuple(every), shard, not raw, SMALL)
        turn = after(me, outs[0])
        packed.update(zip(every, outs))
        raw.append(packed)
    lead = {flip: send(raw[0][flip], flip) for flip in LEAD_ORDER}
    lead = [lead[flip] for flip in every]
    slab_incoming = send(after(slab_given, raw[1][0]), ALONG, 2, "replica")
    updated, velocity = outer_update(slab_kept, slab_incoming, global_weights, outer_momentum)
    rest = [send(raw[1][flip], flip) for flip in every]

    sums = product(me, cot, act, lead, lead, GROUPS[0], shard)
    one = {tile: send(sums[tile][0], TILES[tile][1]) for tile in GROUPS[0]}
    sums.update(product(me, cot, act, lead, rest, GROUPS[1], shard))
    updated_other = send(updated, ALONG, 2, "replica")
    one.update({tile: send(sums[tile][0], TILES[tile][1]) for tile in GROUPS[1]})

    two, three = {}, {}
    for tile, (_, _, second) in enumerate(TILES):
        given = sums[tile][1][:, 2 * LANES :] + one[tile][:, 2 * LANES :]
        two[tile] = send(given, second)
    pair = outer_pair(updated, updated_other)
    pair_other = send(pair, ACROSS, 1, "replica")
    alike = {}
    for tile, flips in enumerate(TILES):
        alike.setdefault(flips, []).append(tile)
    for (_, _, second), tiles in alike.items():
        given = []
        for tile in tiles:
            part = slice(LANES, 2 * LANES)
            given.append(sums[tile][1][:, part] + one[tile][:, part] + two[tile][:, part])
        given = given[0] if len(given) == 1 else jnp.concatenate(given, axis=1)
        arrived = send(given, second, far_flip(tiles[0]))
        three.update({tile: (arrived, n * LANES) for n, tile in enumerate(tiles)})
    anchor = outer_whole(pair, pair_other)
    global_out, momentum_out = updated.T, velocity.T

    outs = []
    for tiles in FINISH:
        parts = [
            ((sums[tile][1], 0), (one[tile], 0), (two[tile], 0), three[tile]) for tile in tiles
        ]
        outs = step(parts, current, first_moment[0], second_moment[0], anchor, outs, tiles)
    mixed_weights, first_out, second_out = outs
    return (mixed_weights[None], first_out[None], second_out[None], global_out, momentum_out)


def solution(mesh):
    return jax.shard_map(
        body,
        mesh=mesh,
        in_specs=(
            P("replica", "fsdp", None),
            P("replica", "fsdp", None),
            P("replica", "fsdp", None),
            P("replica", "fsdp", None),
            P("replica", "fsdp", None),
            P("fsdp", "replica"),
            P("fsdp", "replica"),
        ),
        out_specs=(
            P("replica", "fsdp", None),
            P("replica", "fsdp", None),
            P("replica", "fsdp", None),
            P("fsdp", "replica"),
            P("fsdp", "replica"),
        ),
        check_vma=False,
    )
```

```python
import functools

import jax
import jax.numpy as jnp
from jax import lax
from jax.experimental import pallas as pl
from jax.experimental.pallas import tpu as pltpu
from jax.sharding import PartitionSpec as P

BETA_ONE = 0.9
BETA_TWO = 0.95
INNER_RATE = 0.05
EPSILON = 1e-08
DECAY = 0.1
OUTER_RATE = 0.7
NESTEROV = 0.9
MIXING = 0.5

LANES = 128
HUBS = 8
FLIPS = (1, 3, 8, 24, 4)
TILES = (((0, 1, 2), 3, 4), ((3, 4, 0), 1, 2), ((1, 2, 3), 4, 0), ((2, 3, 4), 0, 1), ((4, 0, 1), 2, 3), ((0, 1, 2), 3, 4), ((3, 4, 0), 1, 2))
GROUPS = ((0, 1, 2, 3), (4, 5, 6))
FIRST_ORDER = ((0, 1, 2, 3), (4, 6, 5))
SECOND_ORDER = (0, 1, 2, 3, 4, 5, 6)
THIRD_ORDER = ((1, 6), (0, 5), (2,), (3,), (4,))
FINISH = ((0, 5), (2, 3, 4, 1, 6))
PACKS = ((0, 1, 2, 3, 4),)
LEAD_ORDER = (2, 4, 1, 3, 0)
REST_ORDER = (3, 1, 0, 4, 2)
SHARE_AFTER = -2
ALONG = 4
ALONG_CHAINED = True
UPDATE_LATE = False
BACK = 4
BACK_CHAINED = True
ACROSS = 1
ACROSS_CHAINED = False
BACK_PLACE = 0
PAIR_PLACE = 8
SECOND_TIED = False
SECOND_LATE = False
SECOND_CHAINED = True
THIRD_TIED = False
THIRD_CHAINED = True
PACK_COST = (1, 10000000)
PRODUCT_COST = 1
STEP_COST = 10000000


def cost_of(size):
    return pl.CostEstimate(flops=1, bytes_accessed=size, transcendentals=0)


VMEM_LIMIT = 60 * 1024 * 1024


def flip_pairs(flip, count):
    return [(index, index ^ flip) for index in range(count)]


def far_flip(tile):
    one, two, three = TILES[tile][0]
    return FLIPS[one] ^ FLIPS[two] ^ FLIPS[three]


def hubs(tile):
    _, first, second = TILES[tile]
    return [
        (far_flip(tile) if j & 1 else 0)
        ^ (FLIPS[second] if j & 2 else 0)
        ^ (FLIPS[first] if j & 4 else 0)
        for j in range(HUBS)
    ]


def carried(group, flip):
    return [tile for tile in group if flip in TILES[tile][0]]


def columns(me, flip, tile, hub, shard):
    start = (me ^ (flip ^ hub)) * shard + tile * LANES
    return pl.ds(pl.multiple_of(start, LANES), LANES)


def pack_kernel(me_ref, cot_ref, act_ref, *refs, group, flips, shard, with_act):
    count = len(flips)
    outs, stages, sem, out_sem = refs[:count], refs[count : 2 * count], refs[-2], refs[-1]
    started = []
    for n, flip in enumerate(flips):
        copies = []
        for tile in carried(group, flip):
            for hub in hubs(tile):
                at = len(copies)
                copies.append(
                    pltpu.make_async_copy(
                        cot_ref.at[:, columns(me_ref[0], FLIPS[flip], tile, hub, shard)],
                        stages[n].at[:, pl.ds(at * LANES, LANES)],
                        sem.at[n, at],
                    )
                )
        if with_act:
            at = len(copies)
            copies.append(
                pltpu.make_async_copy(
                    act_ref,
                    stages[n].at[:, pl.ds(at * LANES, act_ref.shape[1])],
                    sem.at[n, at],
                )
            )
        for copy in copies:
            copy.start()
        started.append(copies)
    stores = []
    for n, copies in enumerate(started):
        for copy in copies:
            copy.wait()
        stores.append(pltpu.make_async_copy(stages[n], outs[n], out_sem.at[n]))
        stores[-1].start()
    for store in stores:
        store.wait()


def pack(me, cot, act, group, flips, shard, with_act, cost):
    tokens, features = act.shape
    extra = features if with_act else 0
    shapes = [(tokens, len(carried(group, flip)) * HUBS * LANES + extra) for flip in flips]
    return pl.pallas_call(
        functools.partial(
            pack_kernel, group=group, flips=flips, shard=shard, with_act=with_act
        ),
        out_shape=[jax.ShapeDtypeStruct(shape, jnp.float32) for shape in shapes],
        in_specs=[
            pl.BlockSpec(memory_space=pltpu.SMEM),
            pl.BlockSpec(memory_space=pl.ANY),
            pl.BlockSpec(memory_space=pl.ANY),
        ],
        out_specs=[pl.BlockSpec(memory_space=pl.ANY)] * len(flips),
        scratch_shapes=[pltpu.VMEM(shape, jnp.float32) for shape in shapes]
        + [
            pltpu.SemaphoreType.DMA((len(flips), len(group) * HUBS + 1)),
            pltpu.SemaphoreType.DMA((len(flips),)),
        ],
        compiler_params=pltpu.CompilerParams(vmem_limit_bytes=VMEM_LIMIT),
        cost_estimate=cost,
        name="pack_raw",
    )(me, cot, act)


def product_kernel(me_ref, cot_ref, act_ref, *refs, group, shard, first):
    count, flips = len(group), len(FLIPS)
    lead = refs[:flips]
    refs = refs[flips:]
    messages = lead
    if not first:
        messages, refs = refs[:flips], refs[flips:]
    outs, refs = refs[: 2 * count], refs[2 * count :]
    acts, terms, results, high, low, act_sem, term_sem, out_sem = refs
    tokens, features = act_ref.shape

    loads = [pltpu.make_async_copy(act_ref, acts.at[0], act_sem.at[0])]
    for flip in range(flips):
        width = lead[flip].shape[1]
        loads.append(
            pltpu.make_async_copy(
                lead[flip].at[:, pl.ds(width - features, features)],
                acts.at[flip + 1],
                act_sem.at[flip + 1],
            )
        )
    for load in loads:
        load.start()
    fetches = []
    for n, tile in enumerate(group):
        copies = []
        for j, hub in enumerate(hubs(tile)):
            copies.append(
                pltpu.make_async_copy(
                    cot_ref.at[:, columns(me_ref[0], 0, tile, hub, shard)],
                    terms.at[n, pl.ds(0, tokens), pl.ds(j * LANES, LANES)],
                    term_sem.at[n, j],
                )
            )
        for k, flip in enumerate(TILES[tile][0]):
            place = carried(group, flip).index(tile)
            copies.append(
                pltpu.make_async_copy(
                    messages[flip].at[:, pl.ds(place * HUBS * LANES, HUBS * LANES)],
                    terms.at[n, pl.ds((k + 1) * tokens, tokens), :],
                    term_sem.at[n, HUBS + k],
                )
            )
        for copy in copies:
            copy.start()
        fetches.append(copies)
    for load in loads:
        load.wait()
    for k in range(flips + 1):
        turned = acts[k].T
        rounded = turned.astype(jnp.bfloat16)
        high[k] = rounded
        low[k] = (turned - rounded.astype(jnp.float32)).astype(jnp.bfloat16)

    stores = []
    for n, tile in enumerate(group):
        picks = [0] + [flip + 1 for flip in TILES[tile][0]]
        left_high = jnp.concatenate([high[k] for k in picks], axis=1)
        left_low = jnp.concatenate([low[k] for k in picks], axis=1)
        left = jnp.concatenate([left_high, left_low], axis=0)
        for copy in fetches[n]:
            copy.wait()
        for half in range(2):
            chunk = HUBS * LANES // 2
            term = terms[n, :, pl.ds((1 - half) * chunk, chunk)]
            top = term.astype(jnp.bfloat16)
            rest = (term - top.astype(jnp.float32)).astype(jnp.bfloat16)
            both = jnp.dot(left, top, preferred_element_type=jnp.float32)
            total = jnp.dot(left_high, rest, preferred_element_type=jnp.float32)
            results[n, half] = both[:features] + (both[features:] + total)
            stores.append(
                pltpu.make_async_copy(
                    results.at[n, half], outs[2 * n + half], out_sem.at[n, half]
                )
            )
            stores[-1].start()
    for store in stores:
        store.wait()


def product(me, cot, act, lead, messages, group, shard):
    tokens, features = act.shape
    count = len(group)
    chunk = HUBS * LANES // 2
    operands = [me, cot, act, *lead] + ([] if messages is lead else list(messages))
    out = pl.pallas_call(
        functools.partial(
            product_kernel, group=group, shard=shard, first=messages is lead
        ),
        out_shape=[jax.ShapeDtypeStruct((features, chunk), jnp.float32)] * (2 * count),
        in_specs=[pl.BlockSpec(memory_space=pltpu.SMEM)]
        + [pl.BlockSpec(memory_space=pl.ANY)] * (len(operands) - 1),
        out_specs=[pl.BlockSpec(memory_space=pl.ANY)] * (2 * count),
        scratch_shapes=[
            pltpu.VMEM((len(FLIPS) + 1, tokens, features), jnp.float32),
            pltpu.VMEM((count, 4 * tokens, HUBS * LANES), jnp.float32),
            pltpu.VMEM((count, 2, features, chunk), jnp.float32),
            pltpu.VMEM((len(FLIPS) + 1, features, tokens), jnp.bfloat16),
            pltpu.VMEM((len(FLIPS) + 1, features, tokens), jnp.bfloat16),
            pltpu.SemaphoreType.DMA((len(FLIPS) + 1,)),
            pltpu.SemaphoreType.DMA((count, HUBS + 3)),
            pltpu.SemaphoreType.DMA((count, 2)),
        ],
        compiler_params=pltpu.CompilerParams(vmem_limit_bytes=VMEM_LIMIT),
        cost_estimate=cost_of(PRODUCT_COST),
        name="gradient_terms",
    )(*operands)
    return {tile: (out[2 * n], out[2 * n + 1]) for n, tile in enumerate(group)}


def step_kernel(*refs, tiles, places):
    count = len(tiles)
    part_refs, refs = refs[: 4 * count], refs[4 * count :]
    row_refs, anchor_ref, refs = refs[:3], refs[3], refs[4:]
    outs, (parts, rows, anchors, results, in_sem, out_sem) = refs[-9:-6], refs[-6:]
    fetches = []
    for n, tile in enumerate(tiles):
        span = pl.ds(tile * LANES, LANES)
        copies = [
            pltpu.make_async_copy(ref.at[span, :], rows.at[n, k], in_sem.at[n, k])
            for k, ref in enumerate(row_refs)
        ]
        copies.append(
            pltpu.make_async_copy(anchor_ref.at[:, span], anchors.at[n], in_sem.at[n, 3])
        )
        for k in range(4):
            copies.append(
                pltpu.make_async_copy(
                    part_refs[4 * n + k].at[:, pl.ds(places[n][k], LANES)],
                    parts.at[n, k],
                    in_sem.at[n, 4 + k],
                )
            )
        for copy in copies:
            copy.start()
        fetches.append(copies)
    stores = []
    for n, tile in enumerate(tiles):
        for copy in fetches[n]:
            copy.wait()
        gradient = (parts[n, 0] + parts[n, 1] + (parts[n, 2] + parts[n, 3])).T
        current = rows[n, 0]
        moment = BETA_ONE * rows[n, 1] + (1.0 - BETA_ONE) * gradient
        spread = BETA_TWO * rows[n, 2] + (1.0 - BETA_TWO) * gradient * gradient
        stepped = current - INNER_RATE * (
            moment / (jnp.sqrt(spread) + EPSILON) + DECAY * current
        )
        results[n, 0] = MIXING * stepped + (1.0 - MIXING) * anchors[n].T
        results[n, 1] = moment
        results[n, 2] = spread
        for k in range(3):
            stores.append(
                pltpu.make_async_copy(
                    results.at[n, k], outs[k].at[pl.ds(tile * LANES, LANES), :], out_sem.at[n, k]
                )
            )
            stores[-1].start()
    for store in stores:
        store.wait()


def step(parts, weight, first, second, anchor, previous, tiles):
    rows, features = weight.shape
    count = len(tiles)
    operands = [array for group in parts for array, _ in group]
    operands += [weight, first, second, anchor]
    places = [[place for _, place in group] for group in parts]
    return pl.pallas_call(
        functools.partial(step_kernel, tiles=tiles, places=places),
        out_shape=[jax.ShapeDtypeStruct((rows, features), jnp.float32)] * 3,
        in_specs=[pl.BlockSpec(memory_space=pl.ANY)] * (len(operands) + len(previous)),
        out_specs=[pl.BlockSpec(memory_space=pl.ANY)] * 3,
        input_output_aliases={len(operands) + k: k for k in range(len(previous))},
        scratch_shapes=[
            pltpu.VMEM((count, 4, features, LANES), jnp.float32),
            pltpu.VMEM((count, 3, LANES, features), jnp.float32),
            pltpu.VMEM((count, features, LANES), jnp.float32),
            pltpu.VMEM((count, 3, LANES, features), jnp.float32),
            pltpu.SemaphoreType.DMA((count, 8)),
            pltpu.SemaphoreType.DMA((count, 3)),
        ],
        compiler_params=pltpu.CompilerParams(vmem_limit_bytes=VMEM_LIMIT),
        cost_estimate=cost_of(STEP_COST),
        name="inner_step",
    )(*operands, *previous)


def after(value, *earlier):
    return lax.optimization_barrier((value, *earlier))[0]


def outer_share(current, slab, *earlier):
    core = lax.axis_index("replica") % 2
    turned = current.T.reshape(2, 2, slab, -1)
    kept = lax.dynamic_index_in_dim(turned, core, 1, keepdims=False)
    given = lax.dynamic_index_in_dim(turned, 1 - core, 1, keepdims=False)
    pair = kept + lax.ppermute(after(given, *earlier), "replica", flip_pairs(1, 4))
    far = lax.axis_index("replica") // 2
    kept = lax.dynamic_index_in_dim(pair, far, 0, keepdims=False)
    return kept, lax.dynamic_index_in_dim(pair, 1 - far, 0, keepdims=False), given


def outer_update(kept, incoming, global_weights, outer_momentum):
    summed = kept + incoming
    anchor = global_weights.T
    pseudo_grad = anchor - summed / 4
    velocity = NESTEROV * outer_momentum.T + pseudo_grad
    updated = anchor - OUTER_RATE * (pseudo_grad + NESTEROV * velocity)
    return updated, velocity


def outer_pair(updated, other):
    far = lax.axis_index("replica") // 2
    return jnp.stack([jnp.where(far == 0, updated, other), jnp.where(far == 0, other, updated)])


def outer_whole(pair, other):
    core = lax.axis_index("replica") % 2
    full = jnp.stack(
        [jnp.where(core == 0, pair, other), jnp.where(core == 0, other, pair)], axis=1
    )
    return full.reshape(-1, pair.shape[-1])


def body(
    activations, cotangent, weights, first_moment, second_moment, global_weights, outer_momentum
):
    act, cot, current = activations[0], cotangent[0], weights[0]
    shard = current.shape[0]
    assert shard == len(TILES) * LANES
    me = lax.axis_index("fsdp").astype(jnp.int32).reshape(1)
    every = range(len(FLIPS))
    last = [None] * len(FLIPS)

    def send(value, flip, mask=None, axis="fsdp", chained=True):
        if chained and last[flip] is not None:
            value = after(value, last[flip])
        mask = FLIPS[flip] if mask is None else mask
        arrived = lax.ppermute(value, axis, flip_pairs(mask, lax.axis_size(axis)))
        if chained:
            last[flip] = arrived
        return arrived

    slab = global_weights.shape[1]
    turn = me
    if SHARE_AFTER < 0:
        slab_kept, slab_given, turned = outer_share(current, slab)
        if SHARE_AFTER == -1:
            turn = after(me, turned)
    raw = []
    for group in GROUPS:
        packed = {}
        for flips in PACKS if not raw else (tuple(every),):
            cost = cost_of(PACK_COST[len(raw)])
            outs = pack(turn, cot, act, group, flips, shard, not raw, cost)
            turn = after(me, outs[0])
            packed.update(zip(flips, outs))
        raw.append(packed)
    lead = {flip: send(raw[0][flip], flip) for flip in LEAD_ORDER}
    if SHARE_AFTER >= 0:
        slab_kept, slab_given, _ = outer_share(current, slab, raw[1][0], lead[SHARE_AFTER])
    slab_given = after(slab_given, raw[1][0])
    slab_incoming = send(slab_given, ALONG, 2, "replica", ALONG_CHAINED)
    rest = {flip: send(raw[1][flip], flip) for flip in REST_ORDER}
    lead, rest = [lead[flip] for flip in every], [rest[flip] for flip in every]

    sums = product(me, cot, act, lead, lead, GROUPS[0], shard)
    if UPDATE_LATE:
        slab_incoming = after(slab_incoming, sums[GROUPS[0][0]][1])
    updated, velocity = outer_update(slab_kept, slab_incoming, global_weights, outer_momentum)
    held = {}

    def back(place):
        if place == BACK_PLACE:
            held["other"] = send(updated, BACK, 2, "replica", BACK_CHAINED)
        if place == PAIR_PLACE:
            held["pair"] = outer_pair(updated, held["other"])
            held["whole"] = send(held["pair"], ACROSS, 1, "replica", ACROSS_CHAINED)

    one = {tile: send(sums[tile][0], TILES[tile][1]) for tile in FIRST_ORDER[0]}
    back(0)
    sums.update(product(me, cot, act, lead, rest, GROUPS[1], shard))
    one.update({tile: send(sums[tile][0], TILES[tile][1]) for tile in FIRST_ORDER[1]})
    back(1)

    two, three = {}, {}
    turn = sums[GROUPS[1][0]][1]
    for place, tile in enumerate(SECOND_ORDER):
        arrived = one[tile]
        if SECOND_TIED or (SECOND_LATE and tile in GROUPS[0]):
            arrived = after(arrived, turn)
        given = sums[tile][1][:, 2 * LANES :] + arrived[:, 2 * LANES :]
        if SECOND_TIED:
            turn = given
        two[tile] = send(given, TILES[tile][2], chained=SECOND_CHAINED)
        back(2 + place)
    for tiles in THIRD_ORDER:
        given = []
        for tile in tiles:
            part = slice(LANES, 2 * LANES)
            arrived = after(two[tile], turn) if THIRD_TIED else two[tile]
            given.append(sums[tile][1][:, part] + one[tile][:, part] + arrived[:, part])
        given = given[0] if len(given) == 1 else jnp.concatenate(given, axis=1)
        if THIRD_TIED:
            turn = given
        flip = TILES[tiles[0]][2]
        arrived = send(given, flip, far_flip(tiles[0]), chained=THIRD_CHAINED)
        three.update({tile: (arrived, n * LANES) for n, tile in enumerate(tiles)})
    anchor = outer_whole(held["pair"], held["whole"])
    global_out, momentum_out = updated.T, velocity.T

    outs = []
    for tiles in FINISH:
        parts = [
            ((sums[tile][1], 0), (one[tile], 0), (two[tile], 0), three[tile]) for tile in tiles
        ]
        outs = step(parts, current, first_moment[0], second_moment[0], anchor, outs, tiles)
    mixed_weights, first_out, second_out = outs
    return (mixed_weights[None], first_out[None], second_out[None], global_out, momentum_out)


def solution(mesh):
    return jax.shard_map(
        body,
        mesh=mesh,
        in_specs=(
            P("replica", "fsdp", None),
            P("replica", "fsdp", None),
            P("replica", "fsdp", None),
            P("replica", "fsdp", None),
            P("replica", "fsdp", None),
            P("fsdp", "replica"),
            P("fsdp", "replica"),
        ),
        out_specs=(
            P("replica", "fsdp", None),
            P("replica", "fsdp", None),
            P("replica", "fsdp", None),
            P("fsdp", "replica"),
            P("fsdp", "replica"),
        ),
        check_vma=False,
    )
```

```python
import functools

import jax
import jax.numpy as jnp
from jax import lax
from jax.experimental import pallas as pl
from jax.experimental.pallas import tpu as pltpu
from jax.sharding import PartitionSpec as P

BETA_ONE = 0.9
BETA_TWO = 0.95
INNER_RATE = 0.05
EPSILON = 1e-08
DECAY = 0.1
OUTER_RATE = 0.7
NESTEROV = 0.9
MIXING = 0.5

LANES = 128
HUBS = 8
FLIPS = (1, 3, 8, 24, 4)
TILES = (((0, 1, 2), 3, 4), ((3, 4, 0), 1, 2), ((1, 2, 3), 4, 0), ((2, 3, 4), 0, 1), ((4, 0, 1), 2, 3), ((0, 1, 2), 3, 4), ((3, 4, 0), 1, 2))
GROUPS = ((0, 1, 2, 3), (4, 5, 6))
FIRST_ORDER = ((0, 1, 2, 3), (4, 6, 5))
SECOND_ORDER = (0, 1, 2, 3, 4, 5, 6)
THIRD_ORDER = ((1, 6), (0, 5), (2,), (3,), (4,))
FINISH = ((0, 5), (2, 3, 4, 1, 6))
PACKS = ((0, 1, 2, 3, 4),)
LEAD_ORDER = (2, 4, 1, 3, 0)
REST_ORDER = (3, 1, 0, 4, 2)
SHARE_AFTER = -2
ALONG = 4
ALONG_CHAINED = True
UPDATE_LATE = False
BACK = 4
BACK_CHAINED = True
ACROSS = 1
ACROSS_CHAINED = False
BACK_PLACE = 0
PAIR_PLACE = 8
SECOND_TIED = False
SECOND_LATE = False
SECOND_CHAINED = True
THIRD_TIED = False
THIRD_CHAINED = True
PACK_COST = (1, 10000000)
PRODUCT_COST = 1
STEP_COST = 10000000


def cost_of(size):
    return pl.CostEstimate(flops=1, bytes_accessed=size, transcendentals=0)


VMEM_LIMIT = 60 * 1024 * 1024


def flip_pairs(flip, count):
    return [(index, index ^ flip) for index in range(count)]


def far_flip(tile):
    one, two, three = TILES[tile][0]
    return FLIPS[one] ^ FLIPS[two] ^ FLIPS[three]


def hubs(tile):
    _, first, second = TILES[tile]
    return [
        (far_flip(tile) if j & 1 else 0)
        ^ (FLIPS[second] if j & 2 else 0)
        ^ (FLIPS[first] if j & 4 else 0)
        for j in range(HUBS)
    ]


def carried(group, flip):
    return [tile for tile in group if flip in TILES[tile][0]]


def columns(me, flip, tile, hub, shard):
    start = (me ^ (flip ^ hub)) * shard + tile * LANES
    return pl.ds(pl.multiple_of(start, LANES), LANES)


def pack_kernel(me_ref, cot_ref, act_ref, *refs, group, flips, shard, with_act):
    count = len(flips)
    outs, stages, sem, out_sem = refs[:count], refs[count : 2 * count], refs[-2], refs[-1]
    started = []
    for n, flip in enumerate(flips):
        copies = []
        for tile in carried(group, flip):
            for hub in hubs(tile):
                at = len(copies)
                copies.append(
                    pltpu.make_async_copy(
                        cot_ref.at[:, columns(me_ref[0], FLIPS[flip], tile, hub, shard)],
                        stages[n].at[:, pl.ds(at * LANES, LANES)],
                        sem.at[n, at],
                    )
                )
        if with_act:
            at = len(copies)
            copies.append(
                pltpu.make_async_copy(
                    act_ref,
                    stages[n].at[:, pl.ds(at * LANES, act_ref.shape[1])],
                    sem.at[n, at],
                )
            )
        for copy in copies:
            copy.start()
        started.append(copies)
    stores = []
    for n, copies in enumerate(started):
        for copy in copies:
            copy.wait()
        stores.append(pltpu.make_async_copy(stages[n], outs[n], out_sem.at[n]))
        stores[-1].start()
    for store in stores:
        store.wait()


def pack(me, cot, act, group, flips, shard, with_act, cost):
    tokens, features = act.shape
    extra = features if with_act else 0
    shapes = [(tokens, len(carried(group, flip)) * HUBS * LANES + extra) for flip in flips]
    return pl.pallas_call(
        functools.partial(
            pack_kernel, group=group, flips=flips, shard=shard, with_act=with_act
        ),
        out_shape=[jax.ShapeDtypeStruct(shape, jnp.float32) for shape in shapes],
        in_specs=[
            pl.BlockSpec(memory_space=pltpu.SMEM),
            pl.BlockSpec(memory_space=pl.ANY),
            pl.BlockSpec(memory_space=pl.ANY),
        ],
        out_specs=[pl.BlockSpec(memory_space=pl.ANY)] * len(flips),
        scratch_shapes=[pltpu.VMEM(shape, jnp.float32) for shape in shapes]
        + [
            pltpu.SemaphoreType.DMA((len(flips), len(group) * HUBS + 1)),
            pltpu.SemaphoreType.DMA((len(flips),)),
        ],
        compiler_params=pltpu.CompilerParams(vmem_limit_bytes=VMEM_LIMIT),
        cost_estimate=cost,
        name="pack_raw",
    )(me, cot, act)


def product_kernel(me_ref, cot_ref, act_ref, *refs, group, shard, first):
    count, flips = len(group), len(FLIPS)
    lead = refs[:flips]
    refs = refs[flips:]
    messages = lead
    if not first:
        messages, refs = refs[:flips], refs[flips:]
    outs, refs = refs[: 2 * count], refs[2 * count :]
    acts, terms, results, high, low, act_sem, term_sem, out_sem = refs
    tokens, features = act_ref.shape

    loads = [pltpu.make_async_copy(act_ref, acts.at[0], act_sem.at[0])]
    for flip in range(flips):
        width = lead[flip].shape[1]
        loads.append(
            pltpu.make_async_copy(
                lead[flip].at[:, pl.ds(width - features, features)],
                acts.at[flip + 1],
                act_sem.at[flip + 1],
            )
        )
    for load in loads:
        load.start()
    fetches = []
    for n, tile in enumerate(group):
        copies = []
        for j, hub in enumerate(hubs(tile)):
            copies.append(
                pltpu.make_async_copy(
                    cot_ref.at[:, columns(me_ref[0], 0, tile, hub, shard)],
                    terms.at[n, pl.ds(0, tokens), pl.ds(j * LANES, LANES)],
                    term_sem.at[n, j],
                )
            )
        for k, flip in enumerate(TILES[tile][0]):
            place = carried(group, flip).index(tile)
            copies.append(
                pltpu.make_async_copy(
                    messages[flip].at[:, pl.ds(place * HUBS * LANES, HUBS * LANES)],
                    terms.at[n, pl.ds((k + 1) * tokens, tokens), :],
                    term_sem.at[n, HUBS + k],
                )
            )
        fetches.append(copies)
    for copy in fetches[0]:
        copy.start()
    for load in loads:
        load.wait()
    for k in range(flips + 1):
        turned = acts[k].T
        rounded = turned.astype(jnp.bfloat16)
        high[k] = rounded
        low[k] = (turned - rounded.astype(jnp.float32)).astype(jnp.bfloat16)

    stores = []
    for n, tile in enumerate(group):
        picks = [0] + [flip + 1 for flip in TILES[tile][0]]
        left_high = jnp.concatenate([high[k] for k in picks], axis=1)
        left_low = jnp.concatenate([low[k] for k in picks], axis=1)
        left = jnp.concatenate([left_high, left_low], axis=0)
        for copy in fetches[n + 1] if n + 1 < count else ():
            copy.start()
        for copy in fetches[n]:
            copy.wait()
        for half in range(2):
            chunk = HUBS * LANES // 2
            term = terms[n, :, pl.ds((1 - half) * chunk, chunk)]
            top = term.astype(jnp.bfloat16)
            rest = (term - top.astype(jnp.float32)).astype(jnp.bfloat16)
            both = jnp.dot(left, top, preferred_element_type=jnp.float32)
            total = jnp.dot(left_high, rest, preferred_element_type=jnp.float32)
            results[n, half] = both[:features] + (both[features:] + total)
            stores.append(
                pltpu.make_async_copy(
                    results.at[n, half], outs[2 * n + half], out_sem.at[n, half]
                )
            )
            stores[-1].start()
    for store in stores:
        store.wait()


def product(me, cot, act, lead, messages, group, shard):
    tokens, features = act.shape
    count = len(group)
    chunk = HUBS * LANES // 2
    operands = [me, cot, act, *lead] + ([] if messages is lead else list(messages))
    out = pl.pallas_call(
        functools.partial(
            product_kernel, group=group, shard=shard, first=messages is lead
        ),
        out_shape=[jax.ShapeDtypeStruct((features, chunk), jnp.float32)] * (2 * count),
        in_specs=[pl.BlockSpec(memory_space=pltpu.SMEM)]
        + [pl.BlockSpec(memory_space=pl.ANY)] * (len(operands) - 1),
        out_specs=[pl.BlockSpec(memory_space=pl.ANY)] * (2 * count),
        scratch_shapes=[
            pltpu.VMEM((len(FLIPS) + 1, tokens, features), jnp.float32),
            pltpu.VMEM((count, 4 * tokens, HUBS * LANES), jnp.float32),
            pltpu.VMEM((count, 2, features, chunk), jnp.float32),
            pltpu.VMEM((len(FLIPS) + 1, features, tokens), jnp.bfloat16),
            pltpu.VMEM((len(FLIPS) + 1, features, tokens), jnp.bfloat16),
            pltpu.SemaphoreType.DMA((len(FLIPS) + 1,)),
            pltpu.SemaphoreType.DMA((count, HUBS + 3)),
            pltpu.SemaphoreType.DMA((count, 2)),
        ],
        compiler_params=pltpu.CompilerParams(vmem_limit_bytes=VMEM_LIMIT),
        cost_estimate=cost_of(PRODUCT_COST),
        name="gradient_terms",
    )(*operands)
    return {tile: (out[2 * n], out[2 * n + 1]) for n, tile in enumerate(group)}


def step_kernel(*refs, tiles, places):
    count = len(tiles)
    part_refs, refs = refs[: 4 * count], refs[4 * count :]
    row_refs, anchor_ref, refs = refs[:3], refs[3], refs[4:]
    outs, (parts, rows, anchors, results, in_sem, out_sem) = refs[-9:-6], refs[-6:]
    fetches = []
    for n, tile in enumerate(tiles):
        span = pl.ds(tile * LANES, LANES)
        copies = [
            pltpu.make_async_copy(ref.at[span, :], rows.at[n, k], in_sem.at[n, k])
            for k, ref in enumerate(row_refs)
        ]
        copies.append(
            pltpu.make_async_copy(anchor_ref.at[:, span], anchors.at[n], in_sem.at[n, 3])
        )
        for k in range(4):
            copies.append(
                pltpu.make_async_copy(
                    part_refs[4 * n + k].at[:, pl.ds(places[n][k], LANES)],
                    parts.at[n, k],
                    in_sem.at[n, 4 + k],
                )
            )
        for copy in copies:
            copy.start()
        fetches.append(copies)
    stores = []
    for n, tile in enumerate(tiles):
        for copy in fetches[n]:
            copy.wait()
        gradient = (parts[n, 0] + parts[n, 1] + (parts[n, 2] + parts[n, 3])).T
        current = rows[n, 0]
        moment = BETA_ONE * rows[n, 1] + (1.0 - BETA_ONE) * gradient
        spread = BETA_TWO * rows[n, 2] + (1.0 - BETA_TWO) * gradient * gradient
        stepped = current - INNER_RATE * (
            moment / (jnp.sqrt(spread) + EPSILON) + DECAY * current
        )
        results[n, 0] = MIXING * stepped + (1.0 - MIXING) * anchors[n].T
        results[n, 1] = moment
        results[n, 2] = spread
        for k in range(3):
            stores.append(
                pltpu.make_async_copy(
                    results.at[n, k], outs[k].at[pl.ds(tile * LANES, LANES), :], out_sem.at[n, k]
                )
            )
            stores[-1].start()
    for store in stores:
        store.wait()


def step(parts, weight, first, second, anchor, previous, tiles):
    rows, features = weight.shape
    count = len(tiles)
    operands = [array for group in parts for array, _ in group]
    operands += [weight, first, second, anchor]
    places = [[place for _, place in group] for group in parts]
    return pl.pallas_call(
        functools.partial(step_kernel, tiles=tiles, places=places),
        out_shape=[jax.ShapeDtypeStruct((rows, features), jnp.float32)] * 3,
        in_specs=[pl.BlockSpec(memory_space=pl.ANY)] * (len(operands) + len(previous)),
        out_specs=[pl.BlockSpec(memory_space=pl.ANY)] * 3,
        input_output_aliases={len(operands) + k: k for k in range(len(previous))},
        scratch_shapes=[
            pltpu.VMEM((count, 4, features, LANES), jnp.float32),
            pltpu.VMEM((count, 3, LANES, features), jnp.float32),
            pltpu.VMEM((count, features, LANES), jnp.float32),
            pltpu.VMEM((count, 3, LANES, features), jnp.float32),
            pltpu.SemaphoreType.DMA((count, 8)),
            pltpu.SemaphoreType.DMA((count, 3)),
        ],
        compiler_params=pltpu.CompilerParams(vmem_limit_bytes=VMEM_LIMIT),
        cost_estimate=cost_of(STEP_COST),
        name="inner_step",
    )(*operands, *previous)


def after(value, *earlier):
    return lax.optimization_barrier((value, *earlier))[0]


def outer_share(current, slab, *earlier):
    core = lax.axis_index("replica") % 2
    turned = current.T.reshape(2, 2, slab, -1)
    kept = lax.dynamic_index_in_dim(turned, core, 1, keepdims=False)
    given = lax.dynamic_index_in_dim(turned, 1 - core, 1, keepdims=False)
    pair = kept + lax.ppermute(after(given, *earlier), "replica", flip_pairs(1, 4))
    far = lax.axis_index("replica") // 2
    kept = lax.dynamic_index_in_dim(pair, far, 0, keepdims=False)
    return kept, lax.dynamic_index_in_dim(pair, 1 - far, 0, keepdims=False), given


def outer_update(kept, incoming, global_weights, outer_momentum):
    summed = kept + incoming
    anchor = global_weights.T
    pseudo_grad = anchor - summed / 4
    velocity = NESTEROV * outer_momentum.T + pseudo_grad
    updated = anchor - OUTER_RATE * (pseudo_grad + NESTEROV * velocity)
    return updated, velocity


def outer_pair(updated, other):
    far = lax.axis_index("replica") // 2
    return jnp.stack([jnp.where(far == 0, updated, other), jnp.where(far == 0, other, updated)])


def outer_whole(pair, other):
    core = lax.axis_index("replica") % 2
    full = jnp.stack(
        [jnp.where(core == 0, pair, other), jnp.where(core == 0, other, pair)], axis=1
    )
    return full.reshape(-1, pair.shape[-1])


def body(
    activations, cotangent, weights, first_moment, second_moment, global_weights, outer_momentum
):
    act, cot, current = activations[0], cotangent[0], weights[0]
    shard = current.shape[0]
    assert shard == len(TILES) * LANES
    me = lax.axis_index("fsdp").astype(jnp.int32).reshape(1)
    every = range(len(FLIPS))
    last = [None] * len(FLIPS)

    def send(value, flip, mask=None, axis="fsdp", chained=True):
        if chained and last[flip] is not None:
            value = after(value, last[flip])
        mask = FLIPS[flip] if mask is None else mask
        arrived = lax.ppermute(value, axis, flip_pairs(mask, lax.axis_size(axis)))
        if chained:
            last[flip] = arrived
        return arrived

    slab = global_weights.shape[1]
    turn = me
    if SHARE_AFTER < 0:
        slab_kept, slab_given, turned = outer_share(current, slab)
        if SHARE_AFTER == -1:
            turn = after(me, turned)
    raw = []
    for group in GROUPS:
        packed = {}
        for flips in PACKS if not raw else (tuple(every),):
            cost = cost_of(PACK_COST[len(raw)])
            outs = pack(turn, cot, act, group, flips, shard, not raw, cost)
            turn = after(me, outs[0])
            packed.update(zip(flips, outs))
        raw.append(packed)
    lead = {flip: send(raw[0][flip], flip) for flip in LEAD_ORDER}
    if SHARE_AFTER >= 0:
        slab_kept, slab_given, _ = outer_share(current, slab, raw[1][0], lead[SHARE_AFTER])
    slab_given = after(slab_given, raw[1][0])
    slab_incoming = send(slab_given, ALONG, 2, "replica", ALONG_CHAINED)
    rest = {flip: send(raw[1][flip], flip) for flip in REST_ORDER}
    lead, rest = [lead[flip] for flip in every], [rest[flip] for flip in every]

    sums = product(me, cot, act, lead, lead, GROUPS[0], shard)
    if UPDATE_LATE:
        slab_incoming = after(slab_incoming, sums[GROUPS[0][0]][1])
    updated, velocity = outer_update(slab_kept, slab_incoming, global_weights, outer_momentum)
    held = {}

    def back(place):
        if place == BACK_PLACE:
            held["other"] = send(updated, BACK, 2, "replica", BACK_CHAINED)
        if place == PAIR_PLACE:
            held["pair"] = outer_pair(updated, held["other"])
            held["whole"] = send(held["pair"], ACROSS, 1, "replica", ACROSS_CHAINED)

    one = {tile: send(sums[tile][0], TILES[tile][1]) for tile in FIRST_ORDER[0]}
    back(0)
    sums.update(product(me, cot, act, lead, rest, GROUPS[1], shard))
    one.update({tile: send(sums[tile][0], TILES[tile][1]) for tile in FIRST_ORDER[1]})
    back(1)

    two, three = {}, {}
    turn = sums[GROUPS[1][0]][1]
    for place, tile in enumerate(SECOND_ORDER):
        arrived = one[tile]
        if SECOND_TIED or (SECOND_LATE and tile in GROUPS[0]):
            arrived = after(arrived, turn)
        given = sums[tile][1][:, 2 * LANES :] + arrived[:, 2 * LANES :]
        if SECOND_TIED:
            turn = given
        two[tile] = send(given, TILES[tile][2], chained=SECOND_CHAINED)
        back(2 + place)
    for tiles in THIRD_ORDER:
        given = []
        for tile in tiles:
            part = slice(LANES, 2 * LANES)
            arrived = after(two[tile], turn) if THIRD_TIED else two[tile]
            given.append(sums[tile][1][:, part] + one[tile][:, part] + arrived[:, part])
        given = given[0] if len(given) == 1 else jnp.concatenate(given, axis=1)
        if THIRD_TIED:
            turn = given
        flip = TILES[tiles[0]][2]
        arrived = send(given, flip, far_flip(tiles[0]), chained=THIRD_CHAINED)
        three.update({tile: (arrived, n * LANES) for n, tile in enumerate(tiles)})
    anchor = outer_whole(held["pair"], held["whole"])
    global_out, momentum_out = updated.T, velocity.T

    outs = []
    for tiles in FINISH:
        parts = [
            ((sums[tile][1], 0), (one[tile], 0), (two[tile], 0), three[tile]) for tile in tiles
        ]
        outs = step(parts, current, first_moment[0], second_moment[0], anchor, outs, tiles)
    mixed_weights, first_out, second_out = outs
    return (mixed_weights[None], first_out[None], second_out[None], global_out, momentum_out)


def solution(mesh):
    return jax.shard_map(
        body,
        mesh=mesh,
        in_specs=(
            P("replica", "fsdp", None),
            P("replica", "fsdp", None),
            P("replica", "fsdp", None),
            P("replica", "fsdp", None),
            P("replica", "fsdp", None),
            P("fsdp", "replica"),
            P("fsdp", "replica"),
        ),
        out_specs=(
            P("replica", "fsdp", None),
            P("replica", "fsdp", None),
            P("replica", "fsdp", None),
            P("fsdp", "replica"),
            P("fsdp", "replica"),
        ),
        check_vma=False,
    )
```
